128 devices in a mesh: pipe: 8 (over x, core), mp: 16 (over y, z).
Axes of the slice: x: 4, y: 4, z: 4, core: 2. Of those that a mesh axis runs over, the one named last changes fastest.
Arguments:
- inbox: bfloat16 [8, 2048, 4096], P('pipe', 'mp'), may hold values from -45 to 45
- norm_gain: float32 [8, 4096], P('pipe'), may hold values from 0.5 to 1.5
- w_in: bfloat16 [8, 4096, 3, 6144], P('pipe', None, None, 'mp'), may hold values from -0.09375 to 0.09375
- short_w: float32 [8, 7, 3, 6144], P('pipe', None, None, 'mp'), may hold values from -2 to 2
- long_h: bfloat16 [8, 128, 6144], P('pipe', None, 'mp'), may hold values from -0.5 to 0.5
- skip_gain: float32 [8, 6144], P('pipe', 'mp'), may hold values from -1 to 1
- w_out: bfloat16 [8, 6144, 4096], P('pipe', 'mp'), may hold values from -0.078125 to 0.078125
Outputs:
- next_inbox: bfloat16 [8, 2048, 4096], P('pipe', 'mp')
The draws below stay inside these ranges and needn't reach their ends.
All inputs are finite; a program needn't handle non-finite values.
Results may differ from the reference program's by a relative error of at most 0.015.
Values may be sent and summed in bfloat16 or wider, within the bound.
A program may use at most 320 MiB of HBM per device.

```python
import jax
import jax.numpy as jnp
from jax import lax

DW = 4096
CH = 6144
FILT = 128
KSHORT = 7
LENGTH = 1024
SEQS = 2
SECTIONS = 8
TOKENS = 2048
N_MP = 16


def draw_inbox(key, part):
    keys = jax.random.split(key, 3)
    shape = (SECTIONS, TOKENS, DW)
    base = jax.random.normal(keys[0], shape, jnp.float32)
    row_log = jax.random.uniform(keys[1], (SECTIONS, TOKENS, 1), jnp.float32, jnp.log(0.3), jnp.log(3.0))
    base = jnp.clip(base, -5.0, 5.0)
    col_log = jax.random.uniform(keys[2], (SECTIONS, 1, DW), jnp.float32, jnp.log(0.3), jnp.log(3.0))
    return (base * jnp.exp(row_log) * jnp.exp(col_log)).astype(jnp.bfloat16)


def shard_levels(stream_key, extent, cuts, least, top_value):
    loudness = 1.0
    for dim, blocks in cuts:
        steps = jax.random.uniform(jax.random.fold_in(jax.random.fold_in(stream_key, 6), dim), (blocks,), jnp.float32, least / len(cuts), top_value / len(cuts))
        loudness = loudness * jnp.repeat(jnp.exp(steps), extent[dim] // blocks).reshape((-1,) + (1,) * (len(extent) - 1 - dim))
    return loudness


def bell_draw(key, dims, deviation, most, pieces=(), kind=jnp.bfloat16):
    level = shard_levels(key, dims, pieces, -0.22, 0.18) if pieces else 1.0
    entries = jax.random.normal(key, dims, jnp.float32) * deviation * level
    return jnp.minimum(jnp.maximum(entries, -most), most).astype(kind)


def setup_inputs(seed: int = 0) -> dict:
    key_of = jax.random.split(jax.random.key(seed), 8)
    return {
        "inbox": draw_inbox(jax.random.fold_in(key_of[7], 71), 0),
        "norm_gain": jnp.clip(1.0 + 0.1 * jax.random.normal(key_of[1], (SECTIONS, DW), jnp.float32), 0.5, 1.5),
        "w_in": bell_draw(key_of[2], (SECTIONS, DW, 3, CH), DW ** -0.5, 0.09375, ((0, 8), (3, 16))),
        "short_w": bell_draw(key_of[3], (SECTIONS, KSHORT, 3, CH), KSHORT ** -0.5, 2.0, ((0, 8), (3, 16)), jnp.float32),
        "long_h": bell_draw(key_of[4], (SECTIONS, FILT, CH), FILT ** -0.5, 0.5, ((0, 8), (2, 16))),
        "skip_gain": jnp.clip(jax.random.uniform(key_of[5], (SECTIONS, CH), jnp.float32, -1.0, 1.0) * shard_levels(key_of[5], (SECTIONS, CH), ((0, 8), (1, 16)), -0.4, 0.0), -1.0, 1.0),
        "w_out": bell_draw(key_of[6], (SECTIONS, CH, DW), CH ** -0.5, 0.078125, ((0, 8), (1, 16))),
    }


def section_block(rows, gain, w_in, short_w, long_h, skip_gain, w_out):
    rows_f = rows.astype(jnp.float32)
    scale = lax.rsqrt(lax.optimization_barrier(jnp.mean(rows_f * rows_f, axis=-1, keepdims=True)) + 1e-06)
    normed = (rows_f * scale * gain).astype(jnp.bfloat16)
    proj = jnp.dot(normed, w_in.reshape(DW, 3 * CH), preferred_element_type=jnp.float32).astype(jnp.bfloat16)
    proj = proj.reshape(SEQS, LENGTH, 3 * CH).astype(jnp.float32)
    padded = jnp.pad(proj, ((0, 0), (KSHORT - 1, 0), (0, 0)))
    short_flat = short_w.reshape(KSHORT, 3 * CH)
    featured = jnp.zeros((SEQS, LENGTH, 3 * CH), jnp.float32)
    for j in range(KSHORT):
        featured = featured + short_flat[j] * padded[:, KSHORT - 1 - j:KSHORT - 1 - j + LENGTH]
    query = featured[:, :, :CH]
    keys = featured[:, :, CH:2 * CH]
    values = featured[:, :, 2 * CH:]
    mixed_kv = (keys * values).astype(jnp.bfloat16).astype(jnp.float32)
    taps = long_h.astype(jnp.float32)
    padded_u = jnp.pad(mixed_kv, ((0, 0), (FILT - 1, 0), (0, 0)))

    def tap_step(j, acc):
        piece = lax.dynamic_slice_in_dim(padded_u, FILT - 1 - j, LENGTH, 1)
        return acc + lax.dynamic_index_in_dim(taps, j, 0, keepdims=False) * piece
    filtered = lax.fori_loop(0, FILT, tap_step, jnp.zeros((SEQS, LENGTH, CH), jnp.float32))
    filtered = filtered + skip_gain * mixed_kv
    gated = (query * filtered).astype(jnp.bfloat16).reshape(TOKENS, CH)
    width = CH // N_MP

    def group_step(g, acc):
        left = lax.dynamic_slice_in_dim(gated, g * width, width, 1)
        right = lax.dynamic_slice_in_dim(w_out, g * width, width, 0)
        part = jnp.dot(left, right, preferred_element_type=jnp.float32).astype(jnp.bfloat16)
        part = lax.optimization_barrier(part)
        return acc + part.astype(jnp.float32)
    mixed = lax.fori_loop(0, N_MP, group_step, jnp.zeros((TOKENS, DW), jnp.float32))
    return (rows_f + mixed).astype(jnp.bfloat16)

def reference(inbox, norm_gain, w_in, short_w, long_h, skip_gain, w_out):
    blocks = []
    for section in range(SECTIONS):
        blocks.append(section_block(inbox[section], norm_gain[section], w_in[section], short_w[section], long_h[section], skip_gain[section], w_out[section]))
    stacked = jnp.stack(blocks, axis=0)
    return jnp.roll(stacked, 1, axis=0)
```

```python
import functools

import jax
import jax.numpy as jnp
from jax import lax
from jax.experimental import pallas as pl
from jax.experimental.pallas import tpu as pltpu
from jax.sharding import PartitionSpec as P

MESH = pl.DeviceIdType.MESH
F32 = jnp.float32
BF16 = jnp.bfloat16

ROWS = 128
DW = 4096
CHANS = 384
FILT = 128
KSHORT = 7
SIDE = 4
SEQ_CHUNKS = 8
GATHER_A = 2048
REDUCE_A = 2048
LANES = 128

TOP = (0, ROWS // 2)
BOTTOM = (ROWS // 2, ROWS // 2)
FULL = (0, ROWS)


def message_names():
    names = []
    for group in ["1A", "1B"] + [f"2A{j}" for j in range(4)] + [f"2B{j}" for j in range(4)]:
        names += [(group, kind) for kind in ("n1", "n3", "v1", "v3")]
    for group in [f"R1A{j}" for j in range(4)] + [f"R1B{j}" for j in range(4)] + ["R2A", "R2B"]:
        names += [(group, kind) for kind in ("f1", "f3", "m1", "m3")]
    names += [("pipe", "A"), ("pipe", "B")]
    return {name: index for index, name in enumerate(names)}


NAMES = message_names()


def kernel(
    inbox, gain, w_hbm, short_w, long_h, skip, wo_hbm, out,
    x, w, acc, wo, gated, land_fa, land_fb, land_ma, land_mb, land2_fa, land2_fb, land2_ma, land2_mb,
    win, win3, taps, send_sem, recv_sem, load_sem,
):
    p = lax.axis_index("pipe")
    m = lax.axis_index("mp")
    sections = lax.axis_size("pipe")
    y, z = m // SIDE, m % SIDE
    ys = [y, y + 1 - 2 * (y % 2), (y + 2) % SIDE, SIDE - 1 - y]
    zs = [z, z + 1 - 2 * (z % 2), (z + 2) % SIDE, SIDE - 1 - z]
    after = (p + 1) % sections
    before = (p + sections - 1) % sections

    def device(yy, zz):
        return (p, yy * SIDE + zz)

    neighbours = [device(ys[1], z), device(ys[3], z), device(y, zs[1]), device(y, zs[3]), (after, m), (before, m)]
    barrier = pltpu.get_barrier_semaphore()
    for neighbour in neighbours:
        pl.semaphore_signal(barrier, inc=1, device_id=neighbour, device_id_type=MESH)

    loads = [
        pltpu.make_async_copy(w_hbm.at[i], w.at[:, pl.ds(i * CHANS, CHANS)], load_sem.at[i]) for i in range(3)
    ] + [pltpu.make_async_copy(wo_hbm, wo, load_sem.at[3])]
    for load in loads:
        load.start()

    def region(yy, zz, rows, cols):
        return x.at[yy * SIDE + zz, pl.ds(*rows), pl.ds(*cols)]

    def message(name, src, dst, dev):
        k = NAMES[name]
        return pltpu.make_async_remote_copy(
            src_ref=src, dst_ref=dst, send_sem=send_sem.at[k], recv_sem=recv_sem.at[k],
            device_id=dev, device_id_type=MESH,
        )

    class Ring:
        def __init__(self, group, dim, other, cols):
            self.group, self.dim, self.other, self.cols = group, dim, other, cols
            self.c = ys if dim == "y" else zs
            self.to1 = device(ys[1], z) if dim == "y" else device(y, zs[1])
            self.to3 = device(ys[3], z) if dim == "y" else device(y, zs[3])

        def at(self, k, rows):
            if self.dim == "y":
                return region(self.c[k], self.other, rows, self.cols)
            return region(self.other, self.c[k], rows, self.cols)

    class Gather(Ring):
        def msg(self, kind, k, rows, dev):
            return message((self.group, kind), self.at(k, rows), self.at(k, rows), dev)

        def send(self):
            self.msg("n1", 0, FULL, self.to1).start()
            self.msg("n3", 0, FULL, self.to3).start()

        def forward1(self):
            self.msg("n1", 1, FULL, self.to1).wait_recv()
            self.msg("v3", 1, TOP, self.to3).start()

        def forward3(self):
            self.msg("n3", 3, FULL, self.to3).wait_recv()
            self.msg("v1", 3, BOTTOM, self.to1).start()

        def far(self):
            self.msg("v3", 2, TOP, self.to3).wait_recv()
            self.msg("v1", 2, BOTTOM, self.to1).wait_recv()

        def sent(self):
            self.msg("n1", 0, FULL, self.to1).wait_send()
            self.msg("n3", 0, FULL, self.to3).wait_send()
            self.msg("v3", 1, TOP, self.to3).wait_send()
            self.msg("v1", 3, BOTTOM, self.to1).wait_send()

    class Reduce(Ring):
        def __init__(self, group, dim, other, cols, far, near):
            super().__init__(group, dim, other, cols)
            self.far, self.near = far, near

        def msg(self, kind):
            k, rows, land, dev = {
                "f3": (2, TOP, self.far.at[1], self.to3),
                "f1": (2, BOTTOM, self.far.at[0], self.to1),
                "m1": (1, FULL, self.near.at[0], self.to1),
                "m3": (3, FULL, self.near.at[1], self.to3),
            }[kind]
            return message((self.group, kind), self.at(k, rows), land, dev)

        def send_far(self):
            self.msg("f3").start()
            self.msg("f1").start()

        def merge1(self):
            self.msg("f3").wait_recv()
            here = self.at(1, TOP)
            here[...] = (here[...].astype(F32) + self.far[1].astype(F32)).astype(BF16)
            self.msg("m1").start()

        def merge3(self):
            self.msg("f1").wait_recv()
            here = self.at(3, BOTTOM)
            here[...] = (here[...].astype(F32) + self.far[0].astype(F32)).astype(BF16)
            self.msg("m3").start()

        def merge(self):
            self.merge1()
            self.merge3()

        def total(self, residual=None):
            self.msg("m1").wait_recv()
            self.msg("m3").wait_recv()
            here = self.at(0, FULL)

            def rows16(r, carry):
                rows = pl.ds(pl.multiple_of(r * 16, 16), 16)
                value = here[rows, :].astype(F32) + self.near[0, rows, :].astype(F32) + self.near[1, rows, :].astype(F32)
                if residual is not None:
                    value = value + inbox[rows, pl.ds(*self.cols)].astype(F32)
                here[rows, :] = value.astype(BF16)
                return carry

            lax.fori_loop(0, ROWS // 16, rows16, 0)

        def sent(self):
            for kind in ("f3", "f1", "m1", "m3"):
                self.msg(kind).wait_send()

    gather_a, gather_b = (0, GATHER_A), (GATHER_A, DW - GATHER_A)
    g1a = Gather("1A", "y", z, gather_a)
    g1b = Gather("1B", "z", y, gather_b)
    g2a = [Gather(f"2A{j}", "z", ys[j], gather_a) for j in range(4)]
    g2b = [Gather(f"2B{j}", "y", zs[j], gather_b) for j in range(4)]
    reduce_a, reduce_b = (0, REDUCE_A), (REDUCE_A, DW - REDUCE_A)
    r1a = [Reduce(f"R1A{j}", "z", ys[j], reduce_a, land_fa.at[j], land_ma.at[j]) for j in range(4)]
    r1b = [Reduce(f"R1B{j}", "y", zs[j], reduce_b, land_fb.at[j], land_mb.at[j]) for j in range(4)]
    r2a = Reduce("R2A", "y", z, reduce_a, land2_fa, land2_ma)
    r2b = Reduce("R2B", "z", y, reduce_b, land2_fb, land2_mb)

    def normalize(r, carry):
        rows = pl.ds(pl.multiple_of(r * 16, 16), 16)
        value = inbox[rows, :].astype(F32)
        scale = lax.rsqrt(jnp.mean(value * value, axis=-1, keepdims=True) + 1e-06)
        x[m, rows, :] = (value * scale * gain[...]).astype(BF16)
        return carry

    def project_a(first, zz):
        left = jnp.concatenate(
            [x[first + zz, :, pl.ds(*gather_a)], x[first + SIDE + zz, :, pl.ds(*gather_a)]], axis=0
        )
        part = jnp.dot(left, w[pl.ds(*gather_a), :], preferred_element_type=F32)
        acc[first + zz] += part[:ROWS]
        acc[first + SIDE + zz] += part[ROWS:]

    def project_b(yy):
        def two(k, carry):
            lo = yy * SIDE + 2 * k
            left = x[pl.ds(lo, 2), :, pl.ds(*gather_b)].reshape(2 * ROWS, gather_b[1])
            part = jnp.dot(left, w[pl.ds(*gather_b), :], preferred_element_type=F32)
            acc[lo] += part[:ROWS]
            acc[lo + 1] += part[ROWS:]
            return carry

        lax.fori_loop(0, 2, two, 0)

    def short_filter(first):
        def step(k, carry):
            i = SEQ_CHUNKS - 1 - k // 3
            lane = pl.multiple_of((k % 3) * LANES, LANES)
            chunk = first + i
            prev = jnp.maximum(chunk - 1, first)
            streams = []
            for s in range(3):
                cols = pl.ds(s * CHANS + lane, LANES)
                head = acc[prev, pl.ds(ROWS - 8, 8), cols].astype(BF16).astype(F32)
                win3[s, pl.ds(0, 8), :] = jnp.where(i > 0, head, jnp.zeros_like(head))
                win3[s, pl.ds(8, ROWS), :] = acc[chunk, :, cols].astype(BF16).astype(F32)
                value = short_w[pl.ds(0, 1), cols] * win3[s, pl.ds(8, ROWS), :]
                for j in range(1, KSHORT):
                    value = value + short_w[pl.ds(j, 1), cols] * win3[s, pl.ds(8 - j, ROWS), :]
                streams.append(value)
            acc[chunk, :, pl.ds(lane, LANES)] = streams[0]
            acc[chunk, :, pl.ds(CHANS + lane, LANES)] = (streams[1] * streams[2]).astype(BF16).astype(F32)
            return carry

        lax.fori_loop(0, SEQ_CHUNKS * 3, step, 0)

    def long_filter(first, start, count):
        def step(k, carry):
            i = start + k // 3
            lane = pl.multiple_of((k % 3) * LANES, LANES)
            chunk = first + i
            prev = jnp.maximum(chunk - 1, first)
            lanes = pl.ds(lane, LANES)
            u_cols = pl.ds(CHANS + lane, LANES)
            before_u = acc[prev, :, u_cols]
            win[pl.ds(0, ROWS), :] = jnp.where(i > 0, before_u, jnp.zeros_like(before_u))
            own_u = acc[chunk, :, u_cols]
            win[pl.ds(ROWS, ROWS), :] = own_u
            value = skip[:, lanes] * own_u
            for shift in range(8):
                shifted = win[pl.ds(8 - shift, 2 * ROWS - 8), :]
                for a in range(FILT // 8):
                    base = ROWS - 8 - 8 * a
                    value = value + taps[pl.ds(8 * a + shift, 1), lanes] * shifted[base : base + ROWS]
            gated[chunk, :, lanes] = (acc[chunk, :, lanes] * value).astype(BF16)
            return carry

        lax.fori_loop(0, count * 3, step, 0)

    def mix(yy, pair):
        lo = yy * SIDE + 2 * pair
        left = gated[pl.ds(lo, 2)].reshape(2 * ROWS, CHANS)

        def tile(n, carry):
            cols = pl.ds(pl.multiple_of(n * 1024, 1024), 1024)
            part = jnp.dot(left, wo[:, cols], preferred_element_type=F32).astype(BF16)
            x[lo, :, cols] = part[:ROWS]
            x[lo + 1, :, cols] = part[ROWS:]
            return carry

        lax.fori_loop(0, DW // 1024, tile, 0)

    lax.fori_loop(0, ROWS // 16, normalize, 0)
    pl.semaphore_wait(barrier, len(neighbours))
    g1a.send()
    g1b.send()
    g2a[0].send()
    g2b[0].send()

    def clear(k, carry):
        acc[k] = jnp.zeros((ROWS, 3 * CHANS), F32)
        return carry

    lax.fori_loop(0, SIDE * SIDE, clear, 0)
    taps[...] = long_h[...].astype(F32)
    for load in loads:
        load.wait()

    own = (y // 2) * SEQ_CHUNKS
    other = (1 - y // 2) * SEQ_CHUNKS

    g1a.forward1()
    g2a[1].send()
    g1a.forward3()
    g1b.forward1()
    g2b[1].send()
    g1b.forward3()
    g2b[3].send()
    g2a[0].forward1()
    g2a[0].forward3()
    g1b.far()
    g2b[2].send()
    project_b(y)
    g2a[1].forward1()
    g2a[1].forward3()
    g1a.far()
    g2a[2].send()
    g2a[3].send()
    g2b[0].forward1()
    g2b[0].forward3()
    project_a(other, z)
    g2b[1].forward1()
    g2b[1].forward3()
    g2a[0].far()
    g2a[1].far()
    lax.fori_loop(0, SIDE, lambda zz, c: (project_a(own, zz), c)[1], 0)
    g2b[3].forward1()
    g2b[3].forward3()
    g2a[2].forward1()
    g2a[2].forward3()
    g2b[2].forward1()
    g2b[2].forward3()
    project_b(ys[1])
    short_filter(own)
    long_filter(own, 0, 4)
    g2a[3].forward1()
    g2a[3].forward3()
    long_filter(own, 4, 4)
    project_b(ys[3])
    project_a(other, zs[1])
    project_a(other, zs[3])
    for ring in [g2a[2], g2a[3]] + g2b:
        ring.far()
    for ring in [g1a, g1b] + g2a + g2b:
        ring.sent()

    far_pair, near_pair = 1 - z // 2, z // 2
    mix(y, far_pair)
    r1a[0].send_far()
    mix(ys[1], far_pair)
    r1a[1].send_far()
    project_a(other, zs[2])
    project_b(ys[2])
    mix(y, near_pair)
    mix(ys[1], near_pair)
    r1a[0].merge()
    r1a[1].merge()
    short_filter(other)
    y2_at, y3_at = ys[2] * SIDE - other, ys[3] * SIDE - other
    long_filter(other, y2_at + 2 * far_pair, 2)
    mix(ys[2], far_pair)
    r1b[2].send_far()
    r1b[3].send_far()
    r1a[2].send_far()
    long_filter(other, y3_at + 2 * far_pair, 2)
    mix(ys[3], far_pair)
    r1a[3].send_far()
    long_filter(other, y2_at + 2 * near_pair, 2)
    mix(ys[2], near_pair)
    r1b[1].send_far()
    r1b[0].send_far()
    r1b[2].merge()
    r1b[3].merge()
    long_filter(other, y3_at + 2 * near_pair, 2)
    mix(ys[3], near_pair)
    r1a[2].merge()
    r1a[3].merge()
    r1b[1].merge()
    r1b[0].merge()
    r1a[0].total()
    r1a[1].total()
    r1b[2].total()
    r2b.send_far()
    r1b[3].total()
    r1a[2].total()
    r2a.send_far()
    r1a[3].total()
    r2b.merge3()
    r1b[1].total()
    r2b.merge1()
    r2a.merge1()
    r2a.merge3()
    r1b[0].total()
    r2b.total(inbox)
    hand_b = message(
        ("pipe", "B"), region(y, z, FULL, reduce_b), out.at[:, pl.ds(*reduce_b)], (after, m)
    )
    hand_b.start()
    r2a.total(inbox)
    hand_a = message(
        ("pipe", "A"), region(y, z, FULL, reduce_a), out.at[:, pl.ds(*reduce_a)], (after, m)
    )
    hand_a.start()
    for ring in r1a + r1b + [r2a, r2b]:
        ring.sent()
    hand_a.wait()
    hand_b.wait()


def on_device(inbox, norm_gain, w_in, short_w, long_h, skip_gain, w_out):
    vmem = pl.BlockSpec(memory_space=pltpu.VMEM)
    anywhere = pl.BlockSpec(memory_space=pl.ANY)
    count = len(NAMES)
    wide_a, wide_b = REDUCE_A, DW - REDUCE_A
    result = pl.pallas_call(
        kernel,
        out_shape=jax.ShapeDtypeStruct((ROWS, DW), BF16),
        in_specs=[vmem, vmem, anywhere, vmem, vmem, vmem, anywhere],
        out_specs=anywhere,
        scratch_shapes=[
            pltpu.VMEM((SIDE * SIDE, ROWS, DW), BF16),
            pltpu.VMEM((DW, 3 * CHANS), BF16),
            pltpu.VMEM((SIDE * SIDE, ROWS, 3 * CHANS), F32),
            pltpu.VMEM((CHANS, DW), BF16),
            pltpu.VMEM((SIDE * SIDE, ROWS, CHANS), BF16),
            pltpu.VMEM((4, 2, ROWS // 2, wide_a), BF16),
            pltpu.VMEM((4, 2, ROWS // 2, wide_b), BF16),
            pltpu.VMEM((4, 2, ROWS, wide_a), BF16),
            pltpu.VMEM((4, 2, ROWS, wide_b), BF16),
            pltpu.VMEM((2, ROWS // 2, wide_a), BF16),
            pltpu.VMEM((2, ROWS // 2, wide_b), BF16),
            pltpu.VMEM((2, ROWS, wide_a), BF16),
            pltpu.VMEM((2, ROWS, wide_b), BF16),
            pltpu.VMEM((2 * ROWS, LANES), F32),
            pltpu.VMEM((3, ROWS + 8, LANES), F32),
            pltpu.VMEM((FILT, CHANS), F32),
            pltpu.SemaphoreType.DMA((count,)),
            pltpu.SemaphoreType.DMA((count,)),
            pltpu.SemaphoreType.DMA((4,)),
        ],
        compiler_params=pltpu.CompilerParams(
            collective_id=0, has_side_effects=True, vmem_limit_bytes=62 * 1024 * 1024
        ),
        cost_estimate=pl.CostEstimate(flops=27_000_000_000, bytes_accessed=20_000_000, transcendentals=0),
        name="relay_block",
    )(
        inbox[0],
        norm_gain,
        jnp.transpose(w_in[0], (1, 0, 2)),
        short_w[0].reshape(KSHORT, 3 * CHANS),
        long_h[0],
        skip_gain,
        w_out[0],
    )
    return result[None]


def solution(mesh):
    return jax.shard_map(
        on_device,
        mesh=mesh,
        in_specs=(
            P("pipe", "mp", None),
            P("pipe", None),
            P("pipe", None, None, "mp"),
            P("pipe", None, None, "mp"),
            P("pipe", None, "mp"),
            P("pipe", "mp"),
            P("pipe", "mp", None),
        ),
        out_specs=P("pipe", "mp", None),
        check_vma=False,
    )
```

```python
import functools

import jax
import jax.numpy as jnp
from jax import lax
from jax.experimental import pallas as pl
from jax.experimental.pallas import tpu as pltpu
from jax.sharding import PartitionSpec as P

MESH = pl.DeviceIdType.MESH
F32 = jnp.float32
BF16 = jnp.bfloat16

ROWS = 128
DW = 4096
CHANS = 384
FILT = 128
KSHORT = 7
SIDE = 4
SEQ_CHUNKS = 8
GATHER_A = 1792
REDUCE_A = 2304
LANES = 128
PIECES = 2

TOP = (0, ROWS // 2)
BOTTOM = (ROWS // 2, ROWS // 2)
FULL = (0, ROWS)


def message_names():
    names = []
    for group in ["1A", "1B"] + [f"2A{j}" for j in range(4)] + [f"2B{j}" for j in range(4)]:
        names += [(group, kind) for kind in ("n1", "n3", "v1", "v3")]
    for group in [f"R1A{j}" for j in range(4)] + [f"R1B{j}" for j in range(4)] + [f"R2A{j}" for j in range(PIECES)] + [f"R2B{j}" for j in range(PIECES)]:
        names += [(group, kind) for kind in ("f1", "f3", "m1", "m3")]
    names += [("pipe", f"{half}{j}") for half in "AB" for j in range(PIECES)]
    return {name: index for index, name in enumerate(names)}


NAMES = message_names()


def kernel(
    inbox, gain, w_hbm, short_w, long_h, skip, wo_hbm, out,
    x, w, acc, wo, gated, land_fa, land_fb, land_ma, land_mb, land2_fa, land2_fb, land2_ma, land2_mb,
    win, win3, taps, tails, send_sem, recv_sem, load_sem,
):
    p = lax.axis_index("pipe")
    m = lax.axis_index("mp")
    sections = lax.axis_size("pipe")
    y, z = m // SIDE, m % SIDE
    ys = [y, y + 1 - 2 * (y % 2), (y + 2) % SIDE, SIDE - 1 - y]
    zs = [z, z + 1 - 2 * (z % 2), (z + 2) % SIDE, SIDE - 1 - z]
    after = (p + 1) % sections
    before = (p + sections - 1) % sections

    def device(yy, zz):
        return (p, yy * SIDE + zz)

    neighbours = [device(ys[1], z), device(ys[3], z), device(y, zs[1]), device(y, zs[3]), (after, m), (before, m)]
    barrier = pltpu.get_barrier_semaphore()
    for neighbour in neighbours:
        pl.semaphore_signal(barrier, inc=1, device_id=neighbour, device_id_type=MESH)

    loads = [
        pltpu.make_async_copy(w_hbm.at[i], w.at[:, pl.ds(i * CHANS, CHANS)], load_sem.at[i]) for i in range(3)
    ] + [pltpu.make_async_copy(wo_hbm, wo, load_sem.at[3])]
    for load in loads:
        load.start()

    def region(yy, zz, rows, cols):
        return x.at[yy * SIDE + zz, pl.ds(*rows), pl.ds(*cols)]

    def message(name, src, dst, dev):
        k = NAMES[name]
        return pltpu.make_async_remote_copy(
            src_ref=src, dst_ref=dst, send_sem=send_sem.at[k], recv_sem=recv_sem.at[k],
            device_id=dev, device_id_type=MESH,
        )

    class Ring:
        def __init__(self, group, dim, other, cols):
            self.group, self.dim, self.other, self.cols = group, dim, other, cols
            self.c = ys if dim == "y" else zs
            self.to1 = device(ys[1], z) if dim == "y" else device(y, zs[1])
            self.to3 = device(ys[3], z) if dim == "y" else device(y, zs[3])

        def at(self, k, rows):
            if self.dim == "y":
                return region(self.c[k], self.other, rows, self.cols)
            return region(self.other, self.c[k], rows, self.cols)

    class Gather(Ring):
        def msg(self, kind, k, rows, dev):
            return message((self.group, kind), self.at(k, rows), self.at(k, rows), dev)

        def send(self):
            self.msg("n1", 0, FULL, self.to1).start()
            self.msg("n3", 0, FULL, self.to3).start()

        def forward1(self):
            self.msg("n1", 1, FULL, self.to1).wait_recv()
            self.msg("v3", 1, TOP, self.to3).start()

        def forward3(self):
            self.msg("n3", 3, FULL, self.to3).wait_recv()
            self.msg("v1", 3, BOTTOM, self.to1).start()

        def arrive(self):
            self.msg("n1", 1, FULL, self.to1).wait_recv()
            self.msg("n3", 3, FULL, self.to3).wait_recv()

        def pass1(self):
            self.msg("v3", 1, TOP, self.to3).start()

        def pass3(self):
            self.msg("v1", 3, BOTTOM, self.to1).start()

        def far(self):
            self.msg("v3", 2, TOP, self.to3).wait_recv()
            self.msg("v1", 2, BOTTOM, self.to1).wait_recv()

        def sent_direct(self):
            self.msg("n1", 0, FULL, self.to1).wait_send()
            self.msg("n3", 0, FULL, self.to3).wait_send()

        def sent_forward1(self):
            self.msg("v3", 1, TOP, self.to3).wait_send()

        def sent_forward3(self):
            self.msg("v1", 3, BOTTOM, self.to1).wait_send()

        def sent(self):
            self.sent_direct()
            self.sent_forward1()
            self.sent_forward3()

    class Reduce(Ring):
        def __init__(self, group, dim, other, cols, far, near):
            super().__init__(group, dim, other, cols)
            self.far, self.near = far, near

        def msg(self, kind):
            k, rows, land, dev = {
                "f3": (2, TOP, self.far.at[1], self.to3),
                "f1": (2, BOTTOM, self.far.at[0], self.to1),
                "m1": (1, FULL, self.near.at[0], self.to1),
                "m3": (3, FULL, self.near.at[1], self.to3),
            }[kind]
            return message((self.group, kind), self.at(k, rows), land, dev)

        def send_far(self):
            self.msg("f3").start()
            self.msg("f1").start()

        def merge1(self):
            self.msg("f3").wait_recv()
            here = self.at(1, TOP)
            here[...] = (here[...].astype(F32) + self.far[1].astype(F32)).astype(BF16)
            self.msg("m1").start()

        def merge3(self):
            self.msg("f1").wait_recv()
            here = self.at(3, BOTTOM)
            here[...] = (here[...].astype(F32) + self.far[0].astype(F32)).astype(BF16)
            self.msg("m3").start()

        def merge(self):
            self.merge1()
            self.merge3()

        def total(self, residual=None):
            self.msg("m1").wait_recv()
            self.msg("m3").wait_recv()
            here = self.at(0, FULL)

            def rows16(r, carry):
                rows = pl.ds(pl.multiple_of(r * 16, 16), 16)
                value = here[rows, :].astype(F32) + self.near[0, rows, :].astype(F32) + self.near[1, rows, :].astype(F32)
                if residual is not None:
                    value = value + inbox[rows, pl.ds(*self.cols)].astype(F32)
                here[rows, :] = value.astype(BF16)
                return carry

            lax.fori_loop(0, ROWS // 16, rows16, 0)

        def sent(self):
            for kind in ("f3", "f1", "m1", "m3"):
                self.msg(kind).wait_send()

    gather_a, gather_b = (0, GATHER_A), (GATHER_A, DW - GATHER_A)
    g1a = Gather("1A", "y", z, gather_a)
    g1b = Gather("1B", "z", y, gather_b)
    g2a = [Gather(f"2A{j}", "z", ys[j], gather_a) for j in range(4)]
    g2b = [Gather(f"2B{j}", "y", zs[j], gather_b) for j in range(4)]
    reduce_a, reduce_b = (0, REDUCE_A), (REDUCE_A, DW - REDUCE_A)
    r1a = [Reduce(f"R1A{j}", "z", ys[j], reduce_a, land_fa.at[j], land_ma.at[j]) for j in range(4)]
    r1b = [Reduce(f"R1B{j}", "y", zs[j], reduce_b, land_fb.at[j], land_mb.at[j]) for j in range(4)]
    cut_a, cut_b = reduce_a[1] // PIECES, reduce_b[1] // PIECES
    r2a = [
        Reduce(f"R2A{j}", "y", z, (cut_a * j, cut_a), land2_fa.at[j], land2_ma.at[j]) for j in range(PIECES)
    ]
    r2b = [
        Reduce(f"R2B{j}", "z", y, (REDUCE_A + cut_b * j, cut_b), land2_fb.at[j], land2_mb.at[j])
        for j in range(PIECES)
    ]

    def normalize(r, carry):
        rows = pl.ds(pl.multiple_of(r * 16, 16), 16)
        value = inbox[rows, :].astype(F32)
        scale = lax.rsqrt(jnp.mean(value * value, axis=-1, keepdims=True) + 1e-06)
        x[m, rows, :] = (value * scale * gain[...]).astype(BF16)
        return carry

    def project_a(first, zz):
        left = jnp.concatenate(
            [x[first + zz, :, pl.ds(*gather_a)], x[first + SIDE + zz, :, pl.ds(*gather_a)]], axis=0
        )
        part = jnp.dot(left, w[pl.ds(*gather_a), :], preferred_element_type=F32)
        acc[first + zz] += part[:ROWS]
        acc[first + SIDE + zz] += part[ROWS:]

    def project_columns(*columns):
        for first, zz in columns:
            project_a(first, zz)

    def project_b(yy, pair):
        lo = yy * SIDE + 2 * pair
        left = x[pl.ds(lo, 2), :, pl.ds(*gather_b)].reshape(2 * ROWS, gather_b[1])
        part = jnp.dot(left, w[pl.ds(*gather_b), :], preferred_element_type=F32)
        acc[lo] += part[:ROWS]
        acc[lo + 1] += part[ROWS:]

    def project_row(yy):
        lax.fori_loop(0, 2, lambda pair, c: (project_b(yy, pair), c)[1], 0)

    def keep_tails(first):
        def step(k, carry):
            tails[first + k] = acc[first + k, pl.ds(ROWS - 8, 8), :].astype(BF16).astype(F32)
            return carry

        lax.fori_loop(0, SEQ_CHUNKS, step, 0)

    def short_filter(first, start, stop):
        def step(k, carry):
            i = k // 3
            lane = pl.multiple_of((k % 3) * LANES, LANES)
            chunk = first + i
            prev = jnp.maximum(chunk - 1, first)
            streams = []
            for s in range(3):
                cols = pl.ds(s * CHANS + lane, LANES)
                head = tails[prev, :, cols]
                win3[s, pl.ds(0, 8), :] = jnp.where(i > 0, head, jnp.zeros_like(head))
                win3[s, pl.ds(8, ROWS), :] = acc[chunk, :, cols].astype(BF16).astype(F32)
                value = short_w[s, :, pl.ds(lane, LANES)] * win3[s, pl.ds(8, ROWS), :]
                for j in range(1, KSHORT):
                    value = value + short_w[3 * j + s, :, pl.ds(lane, LANES)] * win3[s, pl.ds(8 - j, ROWS), :]
                streams.append(value)
            acc[chunk, :, pl.ds(lane, LANES)] = streams[0]
            acc[chunk, :, pl.ds(CHANS + lane, LANES)] = (streams[1] * streams[2]).astype(BF16).astype(F32)
            return carry

        lax.fori_loop(start * 3, stop * 3, step, 0)

    def long_filter(first, start, count):
        def step(k, carry):
            i = start + k // 3
            lane = pl.multiple_of((k % 3) * LANES, LANES)
            chunk = first + i
            prev = jnp.maximum(chunk - 1, first)
            lanes = pl.ds(lane, LANES)
            u_cols = pl.ds(CHANS + lane, LANES)
            before_u = acc[prev, :, u_cols]
            win[pl.ds(0, ROWS), :] = jnp.where(i > 0, before_u, jnp.zeros_like(before_u))
            own_u = acc[chunk, :, u_cols]
            win[pl.ds(ROWS, ROWS), :] = own_u
            value = skip[:, lanes] * own_u
            for shift in range(8):
                shifted = win[pl.ds(8 - shift, 2 * ROWS - 8), :]
                for a in range(FILT // 8):
                    base = ROWS - 8 - 8 * a
                    value = value + taps[pl.ds(8 * a + shift, 1), lanes] * shifted[base : base + ROWS]
            gated[chunk, :, lanes] = (acc[chunk, :, lanes] * value).astype(BF16)
            return carry

        lax.fori_loop(0, count * 3, step, 0)

    def mix(yy, first, count, cols):
        lo = yy * SIDE + first
        left = gated[pl.ds(lo, count)].reshape(count * ROWS, CHANS)
        for start in range(cols[0], cols[0] + cols[1], 1024):
            tile = pl.ds(start, min(1024, cols[0] + cols[1] - start))
            part = jnp.dot(left, wo[:, tile], preferred_element_type=F32).astype(BF16)
            for k in range(count):
                x[lo + k, :, tile] = part[k * ROWS : (k + 1) * ROWS]

    lax.fori_loop(0, ROWS // 16, normalize, 0)
    pl.semaphore_wait(barrier, len(neighbours))
    g1a.send()
    g1b.send()
    g2a[0].send()
    g2b[0].send()

    def clear(k, carry):
        acc[k] = jnp.zeros((ROWS, 3 * CHANS), F32)
        return carry

    lax.fori_loop(0, SIDE * SIDE, clear, 0)
    taps[...] = long_h[...].astype(F32)
    for load in loads:
        load.wait()

    own = (y // 2) * SEQ_CHUNKS
    other = (1 - y // 2) * SEQ_CHUNKS

    far_pair, near_pair = 1 - z // 2, z // 2

    def start_of(row, first):
        return row * SIDE - first

    from2 = start_of(ys[2], other)
    lo = from2 + 2 * far_pair
    need = jnp.maximum(lo - 1, 0)
    hands = []

    def finish(half, k, ring):
        ring.total(inbox)
        hand = message(("pipe", f"{half}{k}"), ring.at(0, FULL), out.at[:, pl.ds(*ring.cols)], (after, m))
        hand.start()
        hands.append(hand)

    g1b.forward1()
    g1a.forward1()
    g1a.forward3()
    g1b.forward3()
    g2b[3].send()
    g2a[0].forward1()
    g2a[1].send()
    g1b.far()
    g2a[3].send()
    g1a.far()
    g2b[1].send()
    project_row(y)
    project_a(other, z)
    g2b[2].send()
    g2a[1].forward3()
    g2a[0].forward3()
    g2a[1].forward1()
    g2b[0].forward3()
    g2a[2].send()
    project_a(own, zs[1])
    g2b[1].forward3()
    g2b[1].forward1()
    project_a(own, zs[3])
    g2b[0].forward1()
    g2a[0].far()
    project_a(own, z)
    g2a[3].forward3()
    g2a[1].far()
    project_b(ys[3], near_pair)
    project_b(ys[1], near_pair)
    g2b[3].forward1()
    g2b[3].forward3()
    project_a(own, zs[2])
    g2a[3].forward1()
    g2b[2].forward1()
    g2b[2].forward3()
    project_b(ys[1], far_pair)
    for ring in [g1a] + g2b:
        ring.sent_direct()
    g1b.sent()
    g2a[0].sent()
    keep_tails(own)
    short_filter(own, 0, SEQ_CHUNKS)
    g2a[2].forward1()
    g2a[2].forward3()
    long_filter(own, start_of(y, own) + 2 * far_pair, 2)
    mix(y, 2 * far_pair, 2, reduce_a)
    r1a[0].send_far()
    g2a[3].far()
    long_filter(own, start_of(y, own) + 2 * near_pair, 2)
    project_a(other, zs[1])
    g2b[0].far()
    mix(y, 2 * near_pair, 2, reduce_a)
    g2b[1].far()
    long_filter(own, start_of(ys[1], own) + 2 * far_pair, 2)
    project_b(ys[2], near_pair)
    r1a[0].merge3()
    g2a[2].far()
    r1a[0].merge1()
    project_a(other, zs[3])
    project_a(other, zs[2])
    project_b(ys[3], far_pair)
    g2a[1].sent()
    g2b[2].sent_forward1()
    g2b[3].sent_forward1()
    g2b[3].far()
    mix(ys[1], 2 * far_pair, 2, reduce_a)
    mix(ys[1], 2 * far_pair, 2, reduce_b)
    g2b[2].far()
    project_b(ys[2], far_pair)
    keep_tails(other)
    short_filter(other, need, lo + 2)
    r1a[1].send_far()
    for ring in g2a[2:]:
        ring.sent()
    g1a.sent_forward3()
    for ring in g2b:
        ring.sent_forward3()
    long_filter(other, from2 + zs[3], 1)
    mix(ys[2], zs[3], 1, reduce_b)
    r1b[3].send_far()
    long_filter(other, from2 + zs[2], 1)
    mix(ys[2], zs[2], 1, reduce_b)
    r1b[2].send_far()
    g1a.sent_forward1()
    g2b[0].sent_forward1()
    g2b[1].sent_forward1()
    mix(ys[2], 2 * far_pair, 2, reduce_a)
    short_filter(other, 0, need)
    short_filter(other, lo + 2, SEQ_CHUNKS)
    long_filter(other, start_of(ys[3], other) + 2 * far_pair, 2)
    mix(ys[3], 2 * far_pair, 2, reduce_b)
    r1a[2].send_far()
    r1b[3].merge1()
    r1b[3].merge3()
    mix(ys[3], 2 * far_pair, 2, reduce_a)
    long_filter(other, start_of(ys[2], other) + 2 * near_pair, 2)
    r1a[3].send_far()
    mix(y, 2 * far_pair, 2, reduce_b)
    mix(ys[2], 2 * near_pair, 2, reduce_b)
    r1a[2].merge3()
    r1b[1].send_far()
    r1b[2].merge3()
    mix(ys[2], 2 * near_pair, 2, reduce_a)
    r1a[2].merge1()
    r1b[2].merge1()
    long_filter(own, start_of(ys[1], own) + 2 * near_pair, 2)
    long_filter(other, start_of(ys[3], other) + 2 * near_pair, 2)
    mix(ys[1], 2 * near_pair, 2, reduce_b)
    mix(ys[3], 2 * near_pair, 2, reduce_a)
    mix(ys[3], 2 * near_pair, 2, reduce_b)
    mix(ys[1], 2 * near_pair, 2, reduce_a)
    mix(y, 2 * near_pair, 2, reduce_b)
    r1a[1].merge3()
    r1b[1].merge1()
    r1b[1].merge3()
    r1a[1].merge1()
    r1b[0].send_far()
    r1a[3].merge3()
    r1b[2].total()
    r1a[3].merge1()
    r1b[3].total()
    r1a[2].total()
    for ring in r2b:
        ring.send_far()
    for ring in r2a:
        ring.send_far()
    r1a[1].total()
    r1b[0].merge3()
    r1b[0].merge1()
    r2a[0].merge1()
    r1a[3].total()
    r1b[1].total()
    r2a[1].merge1()
    r2b[0].merge1()
    r2b[0].merge3()
    r2a[0].merge3()
    r1b[0].total()
    r2b[1].merge3()
    r2a[1].merge3()
    r2b[1].merge1()
    finish("B", 0, r2b[0])
    r1a[0].total()
    finish("A", 0, r2a[0])
    finish("B", 1, r2b[1])
    finish("A", 1, r2a[1])
    for ring in r1a + r1b + r2a + r2b:
        ring.sent()
    for hand in hands:
        hand.wait()


def on_device(inbox, norm_gain, w_in, short_w, long_h, skip_gain, w_out):
    vmem = pl.BlockSpec(memory_space=pltpu.VMEM)
    anywhere = pl.BlockSpec(memory_space=pl.ANY)
    count = len(NAMES)
    wide_a, wide_b = REDUCE_A, DW - REDUCE_A
    result = pl.pallas_call(
        kernel,
        out_shape=jax.ShapeDtypeStruct((ROWS, DW), BF16),
        in_specs=[vmem, vmem, anywhere, vmem, vmem, vmem, anywhere],
        out_specs=anywhere,
        scratch_shapes=[
            pltpu.VMEM((SIDE * SIDE, ROWS, DW), BF16),
            pltpu.VMEM((DW, 3 * CHANS), BF16),
            pltpu.VMEM((SIDE * SIDE, ROWS, 3 * CHANS), F32),
            pltpu.VMEM((CHANS, DW), BF16),
            pltpu.VMEM((SIDE * SIDE, ROWS, CHANS), BF16),
            pltpu.VMEM((4, 2, ROWS // 2, wide_a), BF16),
            pltpu.VMEM((4, 2, ROWS // 2, wide_b), BF16),
            pltpu.VMEM((4, 2, ROWS, wide_a), BF16),
            pltpu.VMEM((4, 2, ROWS, wide_b), BF16),
            pltpu.VMEM((PIECES, 2, ROWS // 2, wide_a // PIECES), BF16),
            pltpu.VMEM((PIECES, 2, ROWS // 2, wide_b // PIECES), BF16),
            pltpu.VMEM((PIECES, 2, ROWS, wide_a // PIECES), BF16),
            pltpu.VMEM((PIECES, 2, ROWS, wide_b // PIECES), BF16),
            pltpu.VMEM((2 * ROWS, LANES), F32),
            pltpu.VMEM((3, ROWS + 8, LANES), F32),
            pltpu.VMEM((FILT, CHANS), F32),
            pltpu.VMEM((SIDE * SIDE, 8, 3 * CHANS), F32),
            pltpu.SemaphoreType.DMA((count,)),
            pltpu.SemaphoreType.DMA((count,)),
            pltpu.SemaphoreType.DMA((4,)),
        ],
        compiler_params=pltpu.CompilerParams(
            collective_id=0, has_side_effects=True, vmem_limit_bytes=62 * 1024 * 1024
        ),
        cost_estimate=pl.CostEstimate(flops=27_000_000_000, bytes_accessed=20_000_000, transcendentals=0),
        name="relay_block",
    )(
        inbox[0],
        norm_gain,
        jnp.transpose(w_in[0], (1, 0, 2)),
        short_w[0].reshape(KSHORT * 3, 1, CHANS),
        long_h[0],
        skip_gain,
        w_out[0],
    )
    return result[None]


def solution(mesh):
    return jax.shard_map(
        on_device,
        mesh=mesh,
        in_specs=(
            P("pipe", "mp", None),
            P("pipe", None),
            P("pipe", None, None, "mp"),
            P("pipe", None, None, "mp"),
            P("pipe", None, "mp"),
            P("pipe", "mp"),
            P("pipe", "mp", None),
        ),
        out_specs=P("pipe", "mp", None),
        check_vma=False,
    )
```

```python
import functools

import jax
import jax.numpy as jnp
from jax import lax
from jax.experimental import pallas as pl
from jax.experimental.pallas import tpu as pltpu
from jax.sharding import PartitionSpec as P

MESH = pl.DeviceIdType.MESH
F32 = jnp.float32
BF16 = jnp.bfloat16

ROWS = 128
DW = 4096
CHANS = 384
FILT = 128
KSHORT = 7
SIDE = 4
SEQ_CHUNKS = 8
GATHER_A = 1920
REDUCE_A = 2176
LANES = 128
PIECES_A = (896, 640, 384, 256)
PIECES_B = (768, 640, 256, 256)

TOP = (0, ROWS // 2)
BOTTOM = (ROWS // 2, ROWS // 2)
FULL = (0, ROWS)


def message_names():
    names = []
    for group in ["1A", "1B"] + [f"2A{j}" for j in range(4)] + [f"2B{j}" for j in range(4)]:
        names += [(group, kind) for kind in ("n1", "n3", "v1", "v3")]
    for group in [f"R1A{j}" for j in range(4)] + [f"R1B{j}" for j in range(4)] + [f"R2A{j}" for j in range(len(PIECES_A))] + [f"R2B{j}" for j in range(len(PIECES_B))]:
        names += [(group, kind) for kind in ("f1", "f3", "m1", "m3")]
    names += [("pipe", f"A{j}") for j in range(len(PIECES_A))] + [("pipe", f"B{j}") for j in range(len(PIECES_B))]
    return {name: index for index, name in enumerate(names)}


NAMES = message_names()


def kernel(
    inbox, gain, w_hbm, short_w, long_h, skip, wo_hbm, out,
    x, w, acc, wo, gated, land_fa, land_fb, land_ma, land_mb, land2_fa, land2_fb, land2_ma, land2_mb,
    win, win3, taps, tails, send_sem, recv_sem, load_sem,
):
    p = lax.axis_index("pipe")
    m = lax.axis_index("mp")
    sections = lax.axis_size("pipe")
    y, z = m // SIDE, m % SIDE
    ys = [y, y + 1 - 2 * (y % 2), (y + 2) % SIDE, SIDE - 1 - y]
    zs = [z, z + 1 - 2 * (z % 2), (z + 2) % SIDE, SIDE - 1 - z]
    after = (p + 1) % sections
    before = (p + sections - 1) % sections

    def device(yy, zz):
        return (p, yy * SIDE + zz)

    neighbours = [device(ys[1], z), device(ys[3], z), device(y, zs[1]), device(y, zs[3]), (after, m), (before, m)]
    barrier = pltpu.get_barrier_semaphore()
    for neighbour in neighbours:
        pl.semaphore_signal(barrier, inc=1, device_id=neighbour, device_id_type=MESH)

    loads = [
        pltpu.make_async_copy(w_hbm.at[i], w.at[:, pl.ds(i * CHANS, CHANS)], load_sem.at[i]) for i in range(3)
    ] + [pltpu.make_async_copy(wo_hbm, wo, load_sem.at[3])]
    for load in loads:
        load.start()

    def region(yy, zz, rows, cols):
        return x.at[yy * SIDE + zz, pl.ds(*rows), pl.ds(*cols)]

    def message(name, src, dst, dev):
        k = NAMES[name]
        return pltpu.make_async_remote_copy(
            src_ref=src, dst_ref=dst, send_sem=send_sem.at[k], recv_sem=recv_sem.at[k],
            device_id=dev, device_id_type=MESH,
        )

    class Ring:
        def __init__(self, group, dim, other, cols):
            self.group, self.dim, self.other, self.cols = group, dim, other, cols
            self.c = ys if dim == "y" else zs
            self.to1 = device(ys[1], z) if dim == "y" else device(y, zs[1])
            self.to3 = device(ys[3], z) if dim == "y" else device(y, zs[3])

        def at(self, k, rows):
            if self.dim == "y":
                return region(self.c[k], self.other, rows, self.cols)
            return region(self.other, self.c[k], rows, self.cols)

    class Gather(Ring):
        def msg(self, kind, k, rows, dev):
            return message((self.group, kind), self.at(k, rows), self.at(k, rows), dev)

        def send(self):
            self.msg("n1", 0, FULL, self.to1).start()
            self.msg("n3", 0, FULL, self.to3).start()

        def forward1(self):
            self.msg("n1", 1, FULL, self.to1).wait_recv()
            self.msg("v3", 1, TOP, self.to3).start()

        def forward3(self):
            self.msg("n3", 3, FULL, self.to3).wait_recv()
            self.msg("v1", 3, BOTTOM, self.to1).start()

        def arrive(self):
            self.msg("n1", 1, FULL, self.to1).wait_recv()
            self.msg("n3", 3, FULL, self.to3).wait_recv()

        def pass1(self):
            self.msg("v3", 1, TOP, self.to3).start()

        def pass3(self):
            self.msg("v1", 3, BOTTOM, self.to1).start()

        def far(self):
            self.msg("v3", 2, TOP, self.to3).wait_recv()
            self.msg("v1", 2, BOTTOM, self.to1).wait_recv()

        def sent_direct(self):
            self.msg("n1", 0, FULL, self.to1).wait_send()
            self.msg("n3", 0, FULL, self.to3).wait_send()

        def sent_forward1(self):
            self.msg("v3", 1, TOP, self.to3).wait_send()

        def sent_forward3(self):
            self.msg("v1", 3, BOTTOM, self.to1).wait_send()

        def sent(self):
            self.sent_direct()
            self.sent_forward1()
            self.sent_forward3()

    class Reduce(Ring):
        def __init__(self, group, dim, other, cols, far, near):
            super().__init__(group, dim, other, cols)
            self.far, self.near = far, near

        def msg(self, kind):
            k, rows, land, dev = {
                "f3": (2, TOP, self.far.at[1], self.to3),
                "f1": (2, BOTTOM, self.far.at[0], self.to1),
                "m1": (1, FULL, self.near.at[0], self.to1),
                "m3": (3, FULL, self.near.at[1], self.to3),
            }[kind]
            return message((self.group, kind), self.at(k, rows), land, dev)

        def send_far(self):
            self.msg("f3").start()
            self.msg("f1").start()

        def merge1(self):
            self.msg("f3").wait_recv()
            here = self.at(1, TOP)
            here[...] = (here[...].astype(F32) + self.far[1].astype(F32)).astype(BF16)
            self.msg("m1").start()

        def merge3(self):
            self.msg("f1").wait_recv()
            here = self.at(3, BOTTOM)
            here[...] = (here[...].astype(F32) + self.far[0].astype(F32)).astype(BF16)
            self.msg("m3").start()

        def merge(self):
            self.merge1()
            self.merge3()

        def total(self, residual=None):
            self.msg("m1").wait_recv()
            self.msg("m3").wait_recv()
            here = self.at(0, FULL)

            def rows16(r, carry):
                rows = pl.ds(pl.multiple_of(r * 16, 16), 16)
                value = here[rows, :].astype(F32) + self.near[0, rows, :].astype(F32) + self.near[1, rows, :].astype(F32)
                if residual is not None:
                    value = value + inbox[rows, pl.ds(*self.cols)].astype(F32)
                here[rows, :] = value.astype(BF16)
                return carry

            lax.fori_loop(0, ROWS // 16, rows16, 0)

        def sent(self):
            for kind in ("f3", "f1", "m1", "m3"):
                self.msg(kind).wait_send()

    gather_a, gather_b = (0, GATHER_A), (GATHER_A, DW - GATHER_A)
    g1a = Gather("1A", "y", z, gather_a)
    g1b = Gather("1B", "z", y, gather_b)
    g2a = [Gather(f"2A{j}", "z", ys[j], gather_a) for j in range(4)]
    g2b = [Gather(f"2B{j}", "y", zs[j], gather_b) for j in range(4)]
    reduce_a, reduce_b = (0, REDUCE_A), (REDUCE_A, DW - REDUCE_A)
    r1a = [Reduce(f"R1A{j}", "z", ys[j], reduce_a, land_fa.at[j], land_ma.at[j]) for j in range(4)]
    r1b = [Reduce(f"R1B{j}", "y", zs[j], reduce_b, land_fb.at[j], land_mb.at[j]) for j in range(4)]
    def last_stage(half, dim, other, first, widths, far, near):
        rings, offset = [], 0
        for j, width in enumerate(widths):
            cols = pl.ds(offset, width)
            ring = Reduce(
                f"R2{half}{j}", dim, other, (first + offset, width), far.at[:, :, cols], near.at[:, :, cols]
            )
            rings.append(ring)
            offset += width
        return rings

    r2a = last_stage("A", "y", z, 0, PIECES_A, land2_fa, land2_ma)
    r2b = last_stage("B", "z", y, REDUCE_A, PIECES_B, land2_fb, land2_mb)

    def normalize(r, carry):
        rows = pl.ds(pl.multiple_of(r * 16, 16), 16)
        value = inbox[rows, :].astype(F32)
        scale = lax.rsqrt(jnp.mean(value * value, axis=-1, keepdims=True) + 1e-06)
        x[m, rows, :] = (value * scale * gain[...]).astype(BF16)
        return carry

    def project_a(first, zz):
        left = jnp.concatenate(
            [x[first + zz, :, pl.ds(*gather_a)], x[first + SIDE + zz, :, pl.ds(*gather_a)]], axis=0
        )
        part = jnp.dot(left, w[pl.ds(*gather_a), :], preferred_element_type=F32)
        acc[first + zz] += part[:ROWS]
        acc[first + SIDE + zz] += part[ROWS:]

    def project_columns(*columns):
        for first, zz in columns:
            project_a(first, zz)

    def project_b(yy, pair):
        lo = yy * SIDE + 2 * pair
        left = x[pl.ds(lo, 2), :, pl.ds(*gather_b)].reshape(2 * ROWS, gather_b[1])
        part = jnp.dot(left, w[pl.ds(*gather_b), :], preferred_element_type=F32)
        acc[lo] += part[:ROWS]
        acc[lo + 1] += part[ROWS:]

    def project_row(yy):
        lax.fori_loop(0, 2, lambda pair, c: (project_b(yy, pair), c)[1], 0)

    def keep_tails(first):
        def step(k, carry):
            tails[first + k] = acc[first + k, pl.ds(ROWS - 8, 8), :].astype(BF16).astype(F32)
            return carry

        lax.fori_loop(0, SEQ_CHUNKS, step, 0)

    def short_filter(first, start, stop):
        def step(k, carry):
            i = k // 3
            lane = pl.multiple_of((k % 3) * LANES, LANES)
            chunk = first + i
            prev = jnp.maximum(chunk - 1, first)
            streams = []
            for s in range(3):
                cols = pl.ds(s * CHANS + lane, LANES)
                head = tails[prev, :, cols]
                win3[s, pl.ds(0, 8), :] = jnp.where(i > 0, head, jnp.zeros_like(head))
                win3[s, pl.ds(8, ROWS), :] = acc[chunk, :, cols].astype(BF16).astype(F32)
                value = short_w[s, :, pl.ds(lane, LANES)] * win3[s, pl.ds(8, ROWS), :]
                for j in range(1, KSHORT):
                    value = value + short_w[3 * j + s, :, pl.ds(lane, LANES)] * win3[s, pl.ds(8 - j, ROWS), :]
                streams.append(value)
            acc[chunk, :, pl.ds(lane, LANES)] = streams[0]
            acc[chunk, :, pl.ds(CHANS + lane, LANES)] = (streams[1] * streams[2]).astype(BF16).astype(F32)
            return carry

        lax.fori_loop(start * 3, stop * 3, step, 0)

    def long_filter(first, start, count):
        def step(k, carry):
            i = start + k // 3
            lane = pl.multiple_of((k % 3) * LANES, LANES)
            chunk = first + i
            prev = jnp.maximum(chunk - 1, first)
            lanes = pl.ds(lane, LANES)
            u_cols = pl.ds(CHANS + lane, LANES)
            before_u = acc[prev, :, u_cols]
            win[pl.ds(0, ROWS), :] = jnp.where(i > 0, before_u, jnp.zeros_like(before_u))
            own_u = acc[chunk, :, u_cols]
            win[pl.ds(ROWS, ROWS), :] = own_u
            value = skip[:, lanes] * own_u
            for shift in range(8):
                shifted = win[pl.ds(8 - shift, 2 * ROWS - 8), :]
                for a in range(FILT // 8):
                    base = ROWS - 8 - 8 * a
                    value = value + taps[pl.ds(8 * a + shift, 1), lanes] * shifted[base : base + ROWS]
            gated[chunk, :, lanes] = (acc[chunk, :, lanes] * value).astype(BF16)
            return carry

        lax.fori_loop(0, count * 3, step, 0)

    def mix(yy, first, count, cols):
        lo = yy * SIDE + first
        left = gated[pl.ds(lo, count)].reshape(count * ROWS, CHANS)
        for start in range(cols[0], cols[0] + cols[1], 1024):
            tile = pl.ds(start, min(1024, cols[0] + cols[1] - start))
            part = jnp.dot(left, wo[:, tile], preferred_element_type=F32).astype(BF16)
            for k in range(count):
                x[lo + k, :, tile] = part[k * ROWS : (k + 1) * ROWS]

    lax.fori_loop(0, ROWS // 16, normalize, 0)
    pl.semaphore_wait(barrier, len(neighbours))
    g1a.send()
    g1b.send()
    g2a[0].send()
    g2b[0].send()

    def clear(k, carry):
        acc[k] = jnp.zeros((ROWS, 3 * CHANS), F32)
        return carry

    lax.fori_loop(0, SIDE * SIDE, clear, 0)
    taps[...] = long_h[...].astype(F32)
    for load in loads:
        load.wait()

    own = (y // 2) * SEQ_CHUNKS
    other = (1 - y // 2) * SEQ_CHUNKS

    far_pair, near_pair = 1 - z // 2, z // 2

    def start_of(row, first):
        return row * SIDE - first

    from2 = start_of(ys[2], other)
    lo = from2 + 2 * far_pair
    need = jnp.maximum(lo - 1, 0)
    hands = []

    def finish(half, k, ring):
        ring.total(inbox)
        hand = message(("pipe", f"{half}{k}"), ring.at(0, FULL), out.at[:, pl.ds(*ring.cols)], (after, m))
        hand.start()
        hands.append(hand)

    g1b.forward1()
    g1a.forward1()
    g1a.forward3()
    g1b.forward3()
    g2b[3].send()
    g2a[1].send()
    g2a[0].forward3()
    g1b.far()
    g2b[2].send()
    g2a[0].forward1()
    g2a[1].forward1()
    project_a(own, z)
    g1a.far()
    g2b[1].send()
    g2a[1].forward3()
    g2a[2].send()
    project_row(y)
    g2b[2].forward3()
    g2b[0].forward3()
    g2b[3].forward3()
    g2a[0].far()
    g2b[2].forward1()
    g2a[1].far()
    project_a(own, zs[2])
    project_a(own, zs[3])
    project_b(ys[3], far_pair)
    project_a(own, zs[1])
    project_a(other, z)
    g2a[3].send()
    g2b[3].forward1()
    project_b(ys[1], far_pair)
    g2a[2].forward3()
    g2b[0].forward1()
    g2a[2].forward1()
    g2b[1].forward1()
    project_b(ys[1], near_pair)
    g2b[1].forward3()
    keep_tails(own)
    short_filter(own, 0, SEQ_CHUNKS)
    long_filter(own, start_of(y, own) + 2 * far_pair, 2)
    for ring in [g1a] + g2b:
        ring.sent_direct()
    g1b.sent()
    g2a[0].sent()
    long_filter(own, start_of(ys[1], own) + 2 * far_pair, 2)
    g2a[3].forward3()
    g2a[3].forward1()
    mix(y, 2 * far_pair, 2, reduce_a)
    g2a[1].sent()
    g2b[2].sent_forward1()
    g2b[3].sent_forward1()
    mix(ys[1], 2 * far_pair, 2, reduce_a)
    r1a[0].send_far()
    project_b(ys[3], near_pair)
    project_a(other, zs[3])
    long_filter(own, start_of(y, own) + 2 * near_pair, 2)
    g2a[3].far()
    g2b[2].far()
    g2b[3].far()
    project_a(other, zs[1])
    r1a[1].send_far()
    g2a[2].far()
    project_b(ys[2], far_pair)
    project_a(other, zs[2])
    g2b[0].far()
    g2b[1].far()
    project_b(ys[2], near_pair)
    keep_tails(other)
    short_filter(other, need, lo + 2)
    for ring in g2a[2:]:
        ring.sent()
    g1a.sent_forward3()
    for ring in g2b:
        ring.sent_forward3()
    long_filter(other, from2 + zs[3], 1)
    mix(ys[2], zs[3], 1, reduce_b)
    r1b[3].send_far()
    mix(y, 2 * near_pair, 2, reduce_a)
    r1a[0].merge1()
    r1a[0].merge3()
    long_filter(other, from2 + zs[2], 1)
    mix(ys[2], zs[2], 1, reduce_b)
    r1b[2].send_far()
    short_filter(other, 0, need)
    short_filter(other, lo + 2, SEQ_CHUNKS)
    long_filter(other, start_of(ys[2], other) + 2 * near_pair, 2)
    mix(ys[2], 2 * near_pair, 2, reduce_b)
    r1b[1].send_far()
    mix(ys[2], 2 * far_pair, 2, reduce_a)
    r1a[2].send_far()
    r1b[0].send_far()
    long_filter(other, start_of(ys[3], other) + 2 * far_pair, 2)
    mix(ys[1], 2 * far_pair, 2, reduce_b)
    mix(ys[3], 2 * far_pair, 2, reduce_a)
    r1b[2].merge1()
    r1b[3].merge1()
    r1a[3].send_far()
    mix(ys[3], 2 * far_pair, 2, reduce_b)
    r1b[2].merge3()
    mix(ys[2], 2 * near_pair, 2, reduce_a)
    r1a[2].merge1()
    g1a.sent_forward1()
    g2b[0].sent_forward1()
    g2b[1].sent_forward1()
    r1a[2].merge3()
    long_filter(other, start_of(ys[3], other) + 2 * near_pair, 2)
    mix(y, 2 * far_pair, 2, reduce_b)
    r1b[3].merge3()
    long_filter(own, start_of(ys[1], own) + 2 * near_pair, 2)
    mix(ys[1], 2 * near_pair, 2, reduce_b)
    r1a[1].merge3()
    mix(ys[3], 2 * near_pair, 2, reduce_b)
    mix(ys[1], 2 * near_pair, 2, reduce_a)
    r1a[1].merge1()
    r1b[0].merge1()
    r1b[1].merge3()
    r1a[2].total()
    r1b[2].total()
    for ring in r2b:
        ring.send_far()
    r1b[1].merge1()
    r1b[3].total()
    for ring in r2a:
        ring.send_far()
    mix(ys[3], 2 * near_pair, 2, reduce_a)
    mix(y, 2 * near_pair, 2, reduce_b)
    r1a[3].merge1()
    r1a[0].total()
    r1a[1].total()
    r1a[3].merge3()
    r1b[0].merge3()
    r2a[0].merge1()
    r2b[1].merge3()
    r1b[1].total()
    r2b[1].merge1()
    r2b[3].merge3()
    r2b[3].merge1()
    r2b[2].merge1()
    r1a[3].total()
    r2a[0].merge3()
    r2b[2].merge3()
    r2a[3].merge1()
    r2b[0].merge3()
    r2b[0].merge1()
    r1b[0].total()
    r2a[1].merge1()
    finish("B", 1, r2b[1])
    r2a[3].merge3()
    finish("B", 3, r2b[3])
    finish("B", 2, r2b[2])
    r2a[1].merge3()
    finish("A", 0, r2a[0])
    r2a[2].merge1()
    r2a[2].merge3()
    finish("A", 3, r2a[3])
    finish("B", 0, r2b[0])
    finish("A", 1, r2a[1])
    finish("A", 2, r2a[2])
    for ring in r1a + r1b + r2a + r2b:
        ring.sent()
    for hand in hands:
        hand.wait()


def on_device(inbox, norm_gain, w_in, short_w, long_h, skip_gain, w_out):
    vmem = pl.BlockSpec(memory_space=pltpu.VMEM)
    anywhere = pl.BlockSpec(memory_space=pl.ANY)
    count = len(NAMES)
    wide_a, wide_b = REDUCE_A, DW - REDUCE_A
    result = pl.pallas_call(
        kernel,
        out_shape=jax.ShapeDtypeStruct((ROWS, DW), BF16),
        in_specs=[vmem, vmem, anywhere, vmem, vmem, vmem, anywhere],
        out_specs=anywhere,
        scratch_shapes=[
            pltpu.VMEM((SIDE * SIDE, ROWS, DW), BF16),
            pltpu.VMEM((DW, 3 * CHANS), BF16),
            pltpu.VMEM((SIDE * SIDE, ROWS, 3 * CHANS), F32),
            pltpu.VMEM((CHANS, DW), BF16),
            pltpu.VMEM((SIDE * SIDE, ROWS, CHANS), BF16),
            pltpu.VMEM((4, 2, ROWS // 2, wide_a), BF16),
            pltpu.VMEM((4, 2, ROWS // 2, wide_b), BF16),
            pltpu.VMEM((4, 2, ROWS, wide_a), BF16),
            pltpu.VMEM((4, 2, ROWS, wide_b), BF16),
            pltpu.VMEM((2, ROWS // 2, wide_a), BF16),
            pltpu.VMEM((2, ROWS // 2, wide_b), BF16),
            pltpu.VMEM((2, ROWS, wide_a), BF16),
            pltpu.VMEM((2, ROWS, wide_b), BF16),
            pltpu.VMEM((2 * ROWS, LANES), F32),
            pltpu.VMEM((3, ROWS + 8, LANES), F32),
            pltpu.VMEM((FILT, CHANS), F32),
            pltpu.VMEM((SIDE * SIDE, 8, 3 * CHANS), F32),
            pltpu.SemaphoreType.DMA((count,)),
            pltpu.SemaphoreType.DMA((count,)),
            pltpu.SemaphoreType.DMA((4,)),
        ],
        compiler_params=pltpu.CompilerParams(
            collective_id=0, has_side_effects=True, vmem_limit_bytes=62 * 1024 * 1024
        ),
        cost_estimate=pl.CostEstimate(flops=27_000_000_000, bytes_accessed=20_000_000, transcendentals=0),
        name="relay_block",
    )(
        inbox[0],
        norm_gain,
        jnp.transpose(w_in[0], (1, 0, 2)),
        short_w[0].reshape(KSHORT * 3, 1, CHANS),
        long_h[0],
        skip_gain,
        w_out[0],
    )
    return result[None]


def solution(mesh):
    return jax.shard_map(
        on_device,
        mesh=mesh,
        in_specs=(
            P("pipe", "mp", None),
            P("pipe", None),
            P("pipe", None, None, "mp"),
            P("pipe", None, None, "mp"),
            P("pipe", None, "mp"),
            P("pipe", "mp"),
            P("pipe", "mp", None),
        ),
        out_specs=P("pipe", "mp", None),
        check_vma=False,
    )
```
